512 devices in a mesh: rho: 8 (over y, z_hi), basis: 64 (over x, z_lo, core).
Axes of the slice: x: 4, y: 4, z: 16 (z_hi: 2, z_lo: 8; z = z_hi * 8 + z_lo), core: 2. Of those that a mesh axis runs over, the one named last changes fastest.
Arguments:
- panels: float32 [8, 49152, 256], P('rho', 'basis'), as said below
- end_panels: float32 [2, 49152, 256], P(None, 'basis'), may hold values from -0.02734375 to 0.02734375
- correlation_diag: float32 [49152], P('basis'), may hold values from 2 to 3
- correlation_band: float32 [3, 49152], P(None, 'basis'), may hold values from -0.3 to 0.3
- band_reach: int32 [49152], P('basis'), may hold values from 1 to 3
- sign_rows: int32 [8, 256], P('rho'), may hold values from 0 to 49151
Outputs:
- couplings: float32 [256, 8, 2, 256], P('basis', 'rho')
The draws below stay inside these ranges and needn't reach their ends.
Inputs may be any that keep to these rules, and one draw needn't show every extreme that they name: panels[k, sign_rows[k, c], c] has magnitude at least 0.5 * 49152 ** -0.5.
All inputs are finite; a program needn't handle non-finite values.
Results may differ from the reference program's by a relative error of at most 0.0003.
Values sent between devices are 32-bit elements; how exact they have to be, the bound alone decides.
No kernel may reach another device: no remote copies, remote signals or barrier semaphores. Data moves between devices by JAX's collectives and lax.ppermute only.
A program may use at most 64 MiB of HBM per device.

```python
import jax
import jax.numpy as jnp
from jax import lax

C = 256
K = 3
NB = 49152
R = 8


def reference_choice(key):
    chosen = jax.random.randint(key, (R, C), 0, NB).astype(jnp.int32)
    chosen = chosen.at[0, 0].set(NB - 1)
    return chosen.at[0, 1].set(0)


def draw_sign_rows(key, part):
    return reference_choice(key)


def draw_panels(key, part):
    chosen = reference_choice(key)
    key = jax.random.fold_in(key, 11)
    first, second, third = jax.random.split(key, 3)
    base = jax.random.normal(first, (R, NB, C), jnp.float32)
    magnitude = jax.random.uniform(second, (R, 1, C), jnp.float32, 0.5, 1.0)
    flip = jax.random.randint(third, (R, 1, C), 0, 2).astype(jnp.float32) * 2.0 - 1.0
    hit = jnp.arange(NB)[None, :, None] == chosen[:, None, :]
    return (jnp.where(hit, magnitude * flip, base) * NB ** (-0.5)).astype(jnp.float32)


def place_ends(values, rng, least, high):
    longest = values.shape.index(max(values.shape))
    spots = []
    for shift in (0, 1):
        where = [jax.random.randint(jax.random.fold_in(rng, axis), (), 0, length) for axis, length in enumerate(values.shape)]
        where[longest] = (where[longest] + shift) % values.shape[longest]
        spots.append(tuple(where))
    return values.at[spots[0]].set(least).at[spots[1]].set(high)


def block_scale(stream_key, shape, shards, smallest, high):
    def one(dim, shards_of):
        steps = jax.random.uniform(jax.random.fold_in(jax.random.fold_in(stream_key, 6), dim), (shards_of,), jnp.float32, smallest / len(shards), high / len(shards))
        return jnp.repeat(jnp.exp(steps), shape[dim] // shards_of).reshape((-1,) + (1,) * (len(shape) - dim - 1))

    gain = one(*shards[0])
    for cut in shards[1:]:
        gain = gain * one(*cut)
    return gain


def noise(key, extent, deviation, bound, cuts=(), held_as=jnp.bfloat16):
    entries = deviation * jax.random.normal(key, extent, jnp.float32)
    if cuts:
        entries = entries * block_scale(key, extent, cuts, -0.22, 0.18)
    return jnp.clip(entries, -bound, bound).astype(held_as)


def setup_inputs(seed: int = 0) -> dict:
    key_list = jax.random.split(jax.random.key(seed), 7)
    return {
        "panels": draw_panels(jax.random.fold_in(key_list[6], 71), 0),
        "end_panels": noise(key_list[1], (2, NB, C), (NB ** -0.5), 0.02734375, ((1, 64),), jnp.float32),
        "correlation_diag": jnp.clip(2.0 + 1.0 * jax.random.uniform(key_list[2], (NB,), jnp.float32) ** block_scale(key_list[2], (NB,), ((0, 64),), -0.2, 0.2), 2.0, 3.0),
        "correlation_band": jnp.clip(jax.random.uniform(key_list[3], (K, NB), jnp.float32, -0.3, 0.3) * block_scale(key_list[3], (K, NB), ((1, 64),), -0.4, 0.0), -0.3, 0.3),
        "band_reach": place_ends(jax.random.randint(key_list[4], (NB,), 1, K + 1), jax.random.fold_in(key_list[4], 1), 1, K).astype(jnp.int32),
        "sign_rows": draw_sign_rows(jax.random.fold_in(key_list[6], 71), 0),
    }


radial_step = 0.5


def apply_correlation(field, correlation_diag, correlation_band, band_reach):
    count = field.shape[0]
    depth = jnp.arange(1, K + 1).astype(jnp.int32)
    band = jnp.where(depth[:, None] <= band_reach[None, :], correlation_band, jnp.float32(0.0))
    padded = jnp.pad(field, ((K, K), (0, 0)))
    band_pad = jnp.pad(band, ((0, 0), (K, 0)))
    result = correlation_diag[:, None] * field
    for depth_step in range(1, K + 1):
        upper = padded[K + depth_step:K + depth_step + count, :]
        lower = padded[K - depth_step:K - depth_step + count, :]
        lower_band = band_pad[depth_step - 1, K - depth_step:K - depth_step + count]
        result = result + band[depth_step - 1][:, None] * upper + lower_band[:, None] * lower
    return result


def reference(panels, end_panels, correlation_diag, correlation_band, band_reach, sign_rows):
    picked = panels[jnp.arange(R)[:, None], sign_rows, jnp.arange(C)[None, :]]
    signs = jnp.sign(picked)

    def one_radius(index):
        below = jnp.maximum(index - 1, 0)
        above = jnp.minimum(index + 1, R - 1)
        current = panels[index] * signs[index][None, :]
        before = jnp.where(index == 0, end_panels[0], panels[below] * signs[below][None, :])
        after = jnp.where(index == R - 1, end_panels[1], panels[above] * signs[above][None, :])
        slope = (after - before) / (2.0 * radial_step)
        applied = apply_correlation(slope, correlation_diag, correlation_band, band_reach)
        drift = jnp.dot(current.T, applied, precision=lax.Precision.HIGHEST)
        curve = jnp.dot(slope.T, applied, precision=lax.Precision.HIGHEST)
        return jnp.stack([drift, curve], axis=1)

    result = lax.map(one_radius, jnp.arange(R).astype(jnp.int32))
    return jnp.transpose(result, (1, 0, 2, 3))
```

```python
import jax
import jax.numpy as jnp
from jax import lax
from jax.sharding import PartitionSpec as P

radial_step = 0.5
edge = 8
both = ("rho", "basis")
exact = lax.Precision.HIGHEST


def hops(target):
    pairs = []
    for rho in range(8):
        for basis in range(64):
            to = target(rho // 2, rho % 2, basis // 16, basis // 2 % 8, basis % 2)
            if to is not None:
                y, h, x, z, core = to
                pairs.append((rho * 64 + basis, (y * 2 + h) * 64 + x * 16 + z * 2 + core))
    return pairs


def basis_step(x, z, core, by):
    index = (x * 16 + z * 2 + core + by) % 64
    return index // 16, index // 2 % 8, index % 2


def move(array, target):
    return lax.ppermute(array, both, hops(target))


x_groups = [[x * 16 + rest for x in range(4)] for rest in range(16)]
z_groups = [[x * 16 + z * 2 + core for z in range(8)] for x in range(4) for core in range(2)]


def spread(array, groups):
    return lax.all_to_all(array, "basis", 0, 0, axis_index_groups=groups)


def gather_sum(vector, groups):
    count = len(groups[0])
    return spread(jnp.broadcast_to(vector[None], (count, *vector.shape)), groups).sum(0)


def swap_core(y, h, x, z, core):
    return y, h, x, z, 1 - core


def swap_parity(y, h, x, z, core):
    return y, 1 - h, x, z, core


def to_neighbour(y, h, x, z, core):
    to = y - 1 if h == 0 else y + 1
    return (to, h, x, z, core) if 0 <= to < 4 else None


def from_neighbour(y, h, x, z, core):
    to = y + 1 if h == 0 else y - 1
    return (to, h, x, z, core) if 0 <= to < 4 else None


def halo_own(y, h, x, z, core):
    return (y, h, *basis_step(x, z, core, 1 if h == 0 else -1))


def halo_visitor(y, h, x, z, core):
    return (y, 1 - h, *basis_step(x, z, core, -1 if h == 0 else 1))


def halo_neighbour(y, h, x, z, core):
    to = (y - 1) % 4 if h == 0 else (y + 1) % 4
    return (to, h, *basis_step(x, z, core, 1 if h == 0 else -1))


def banded(field, diag, band):
    reach, rows = band.shape
    total = diag[:, None] * field
    for d in range(1, reach + 1):
        weight = band[d - 1, : rows - d, None]
        total = total + jnp.pad(weight * field[d:], ((0, d), (0, 0)))
        total = total + jnp.pad(weight * field[: rows - d], ((d, 0), (0, 0)))
    return total


def product(a, b):
    return lax.dot_general(a, b, (((0,), (0,)), ((), ())), precision=exact)


def shards(panels, end_panels, correlation_diag, correlation_band, band_reach, sign_rows):
    own = panels[0]
    rows, width = own.shape
    reach = correlation_band.shape[0]
    half = rows // 2
    rho, basis = lax.axis_index("rho"), lax.axis_index("basis")
    y, h, core = rho // 2, rho % 2, basis % 2
    even = h == 0

    visitor = move(lax.dynamic_slice_in_dim(own, (1 - h) * (half - edge), half + edge), swap_parity)
    near = move(own, to_neighbour)

    local_rows = sign_rows[0] - basis * rows
    hit = lax.broadcasted_iota(jnp.int32, (rows, width), 0) == local_rows[None, :]
    picked = jnp.where(hit, own, 0.0).sum(0)
    depth = jnp.arange(1, reach + 1)[:, None]
    band = jnp.where(depth <= band_reach[None, :], correlation_band, 0.0)

    end_far = jnp.where(even, end_panels[1], end_panels[0])
    end_near = jnp.where(even, end_panels[0], end_panels[1])
    at_far = jnp.where(even, y == 3, y == 0)
    at_near = jnp.where(even, y == 0, y == 3)

    def rim(array):
        return jnp.where(even, array[rows - edge :], array[:edge])

    tail = jnp.pad(band[:, rows - edge :], ((0, edge - reach), (0, width - edge)))
    own_rim = move(jnp.concatenate([rim(own), tail]), halo_own)
    near_rim = move(
        jnp.concatenate(
            [jnp.where(at_near, rim(end_far), rim(own)), jnp.broadcast_to(picked[None], (edge, width))]
        ),
        halo_neighbour,
    )
    visitor_rim = move(
        jnp.concatenate(
            [own[rows - edge :], end_panels[0, rows - edge :], jnp.broadcast_to(picked[None], (edge, width))]
        ),
        halo_visitor,
    )
    probe = jnp.stack([picked, near_rim[edge], visitor_rim[2 * edge]] + [jnp.zeros_like(picked)] * 5)
    probe = probe + move(probe, swap_core)
    probe = gather_sum(probe, x_groups)
    probe = gather_sum(probe, z_groups)
    signs = jnp.sign(probe)
    own_sign, visitor_sign = signs[0], signs[2]
    near_sign = jnp.where(at_far, 1.0, signs[1])

    has_low = even & (basis > 0)
    has_high = (h == 1) & (basis < 63)

    def framed(array, halo):
        return jnp.concatenate([jnp.where(has_low, halo, 0.0), array, jnp.where(has_high, halo, 0.0)])

    own_frame = framed(own, own_rim[:edge]) * own_sign
    near_frame = framed(jnp.where(at_far, end_far, near), near_rim[:edge]) * near_sign
    slope = jnp.where(even, near_frame - own_frame, own_frame - near_frame) / (2.0 * radial_step)
    before = own_rim[edge : edge + reach, :edge]
    inward = jnp.arange(edge)[None, :] + depth >= edge
    band_frame = jnp.concatenate(
        [jnp.where(has_low & inward, before, 0.0), band, jnp.zeros((reach, edge), jnp.float32)], axis=1
    )
    diag_frame = jnp.pad(correlation_diag, (edge, edge))
    applied = banded(slope, diag_frame, band_frame)
    curve = product(slope, applied)

    def window(array, axis=0):
        return lax.dynamic_slice_in_dim(array, h * half, half + 2 * edge, axis)

    place = jnp.arange(half + 2 * edge)[:, None]
    inner = (place >= edge) & (place < edge + half)
    diag_window, band_window = window(diag_frame), window(band_frame, 1)

    def crossed(array):
        source = jnp.where(inner | (h == 1), window(array), 0.0)
        return jnp.where(inner | even, banded(source, diag_window, band_window), 0.0)

    own_applied, near_applied, slope_applied = crossed(own_frame), crossed(near_frame), crossed(slope)

    blank = jnp.zeros((edge, width), jnp.float32)
    seen = jnp.where(
        even, jnp.concatenate([visitor_rim[:edge], visitor]), jnp.concatenate([visitor, blank])
    ) * visitor_sign
    end_frame = jnp.concatenate([visitor_rim[edge : 2 * edge], end_near, blank])
    beside = jnp.where(at_near, window(end_frame), 0.0)
    cross = product(seen, slope_applied)
    first = product(own_applied, (seen - beside) / (2.0 * radial_step))
    second = product(near_applied, seen / (2.0 * radial_step))

    parts = jnp.stack([cross, curve, first, second])
    parts = parts.reshape(4, 4, 8, 2, 4, width).transpose(3, 1, 2, 0, 4, 5).reshape(2, 4, 8, 16, width)
    mine = lax.dynamic_index_in_dim(parts, core, 0, keepdims=False)
    other = lax.dynamic_index_in_dim(parts, 1 - core, 0, keepdims=False)
    mine = mine + move(other, swap_core)
    mine = spread(mine, x_groups).sum(0)
    mine = spread(mine, z_groups).sum(0)
    away, home = mine[:8], mine[8:]
    away = move(away, swap_parity)
    second = move(home, from_neighbour)[4:]
    turn = jnp.where(even, 1.0, -1.0)
    drift = turn * (home[:4] - second) + away[:4]
    curve = away[4:]
    return jnp.stack([drift, curve], axis=1)[:, None]


def solution(mesh):
    in_specs = (
        P("rho", "basis", None),
        P(None, "basis", None),
        P("basis"),
        P(None, "basis"),
        P("basis"),
        P("rho", None),
    )
    out_specs = P("basis", "rho", None, None)
    return jax.shard_map(shards, mesh=mesh, in_specs=in_specs, out_specs=out_specs, check_vma=False)
```

```python
import jax
import jax.numpy as jnp
from jax import lax
from jax.experimental import pallas as pl
from jax.experimental.pallas import tpu as pltpu
from jax.sharding import PartitionSpec as P

radial_step = 0.5
edge = 8
both = ("rho", "basis")
exact = lax.Precision.HIGHEST


def hops(target):
    pairs = []
    for rho in range(8):
        for basis in range(64):
            to = target(rho // 2, rho % 2, basis // 16, basis // 2 % 8, basis % 2)
            if to is not None:
                y, h, x, z, core = to
                pairs.append((rho * 64 + basis, (y * 2 + h) * 64 + x * 16 + z * 2 + core))
    return pairs


def basis_step(x, z, core, by):
    index = (x * 16 + z * 2 + core + by) % 64
    return index // 16, index // 2 % 8, index % 2


def move(array, target):
    return lax.ppermute(array, both, hops(target))


def ring(xs, zs, cores):
    return [x * 16 + z * 2 + core for x in xs for z in zs for core in cores]


quarters = (range(4), range(4, 8))
x_groups = [ring(range(4), (z,), (core,)) for z in range(8) for core in range(2)]
z_groups = [ring((x,), q, (core,)) for x in range(4) for q in quarters for core in range(2)]
cube_groups = [ring(range(4), q, range(2)) for q in quarters]


def spread(array, groups):
    return lax.all_to_all(array, "basis", 0, 0, axis_index_groups=groups)


def swap_core(y, h, x, z, core):
    return y, h, x, z, 1 - core


def swap_quarter(y, h, x, z, core):
    return y, h, x, z ^ 4, core


def swap_parity(y, h, x, z, core):
    return y, 1 - h, x, z, core


def swap_both(y, h, x, z, core):
    return y, 1 - h, x, z ^ 4, core


def to_neighbour(y, h, x, z, core):
    to = y - 1 if h == 0 else y + 1
    return (to, h, x, z, core) if 0 <= to < 4 else None


def from_neighbour(y, h, x, z, core):
    to = y + 1 if h == 0 else y - 1
    return (to, h, x, z, core) if 0 <= to < 4 else None


def halo_own(y, h, x, z, core):
    return (y, h, *basis_step(x, z, core, 1 if h == 0 else -1))


def halo_visitor(y, h, x, z, core):
    return (y, 1 - h, *basis_step(x, z, core, -1 if h == 0 else 1))


def halo_neighbour(y, h, x, z, core):
    to = y - 1 if h == 0 else y + 1
    return (to, h, *basis_step(x, z, core, 1 if h == 0 else -1)) if 0 <= to < 4 else None


def product(a, b):
    return lax.dot_general(
        a, b, (((0,), (0,)), ((), ())), precision=exact, preferred_element_type=jnp.float32
    )


def sign_of(values):
    return jnp.where(values > 0.0, 1.0, jnp.where(values < 0.0, -1.0, 0.0))


def place():
    rho, basis = lax.axis_index("rho"), lax.axis_index("basis")
    return lax.div(rho, 2), lax.rem(rho, 2), basis


def prepare(own, ends_first, ends_last, band, reach, rows_of, out_half, out_rim, out_visitor, out_picked):
    y, h, basis = place()
    rows, width = own.shape
    half = rows // 2
    out_half[...] = own[pl.ds(pl.multiple_of((1 - h) * (half - edge), edge), half + edge), :]
    spot = rows_of[...] - basis * rows
    step = 64
    picked = jnp.zeros((edge, width), jnp.float32)
    for start in range(0, rows, step):
        line = lax.broadcasted_iota(jnp.int32, (step, width), 0) + start
        hit = jnp.where(line == spot, own[start : start + step, :], 0.0)
        picked = picked + hit.reshape(step // edge, edge, width).sum(0)
    picked = jnp.broadcast_to(picked.sum(0, keepdims=True), (edge, width))
    out_picked[...] = jnp.broadcast_to(picked[None], out_picked.shape)
    even = h == 0
    depth = lax.broadcasted_iota(jnp.int32, band.shape, 0) + 1
    masked = jnp.where(depth <= reach[...], band[...], 0.0)
    out_rim[0:edge, :] = jnp.where(even, own[rows - edge :, :], own[:edge, :])
    out_rim[edge : 2 * edge, :] = jnp.zeros((edge, width), jnp.float32)
    out_rim[edge : edge + band.shape[0], :] = masked[:, rows - width :]
    out_rim[2 * edge :, :] = jnp.where(even, ends_last[1], ends_first[0])
    out_visitor[0:edge, :] = own[rows - edge :, :]
    out_visitor[edge:, :] = ends_last[0]


def apply(own, near, ends, own_rim, near_rim, own_sum, near_sum, diag, band, reach,
          out_slope, out_own, out_near, out_curve, own_f, near_f, slope_f, weight_f, turned, applied_f, own_w, near_w, slope_w, weight_w):
    y, h, basis = place()
    rows, width = own.shape
    half = rows // 2
    pad = 2 * edge
    frame = rows + 2 * pad
    even = h == 0
    at_far = (even & (y == 3)) | ((h == 1) & (y == 0))
    far = 1 - h
    own_sign = sign_of(own_sum[0:1, :])
    near_sign = sign_of(near_sum[0:1, :])
    has_low = (even & (basis > 0)).astype(jnp.float32)
    has_high = ((h == 1) & (basis < 63)).astype(jnp.float32)
    blank = jnp.zeros((pad, width), jnp.float32)
    for field in (own_f, near_f):
        field[0:pad, :] = blank
        field[pad + rows :, :] = blank
    own_f[pad : pad + rows, :] = own[...] * own_sign
    own_f[edge:pad, :] = own_rim[0:edge, :] * own_sign * has_low
    own_f[pad + rows : pad + rows + edge, :] = own_rim[0:edge, :] * own_sign * has_high

    @pl.when(at_far)
    def _():
        near_f[pad : pad + rows, :] = ends[far]
        near_f[edge:pad, :] = own_rim[2 * edge :, :] * has_low
        near_f[pad + rows : pad + rows + edge, :] = own_rim[2 * edge :, :] * has_high

    @pl.when(jnp.logical_not(at_far))
    def _():
        near_f[pad : pad + rows, :] = near[...] * near_sign
        near_f[edge:pad, :] = near_rim[0:edge, :] * near_sign * has_low
        near_f[pad + rows : pad + rows + edge, :] = near_rim[0:edge, :] * near_sign * has_high

    turn = jnp.where(even, 1.0, -1.0)
    slope_f[...] = (near_f[...] - own_f[...]) * turn / (2.0 * radial_step)

    count = band.shape[0]
    depth = lax.broadcasted_iota(jnp.int32, band.shape, 0) + 1
    masked = jnp.where(depth <= reach[...], band[...], 0.0)
    lanes = 128
    turned[...] = jnp.zeros(turned.shape, jnp.float32)
    turned[0:1, :] = diag[...]
    turned[edge : edge + count, :] = masked
    weight_f[...] = jnp.zeros(weight_f.shape, jnp.float32)
    for start in range(0, rows, lanes):
        weight_f[pad + start : pad + start + lanes, :] = turned[:, start : start + lanes].T
    before = own_rim[edge : 2 * edge, width - lanes :]
    lane = lax.broadcasted_iota(jnp.int32, before.shape, 1)
    level = lax.broadcasted_iota(jnp.int32, before.shape, 0) + 1
    before = jnp.where(lane + level >= lanes, before, 0.0) * has_low
    turned[edge : 2 * edge, 0:lanes] = before
    turned[0:edge, 0:lanes] = jnp.zeros((edge, lanes), jnp.float32)
    weight_f[edge:pad, :] = turned[:, 0:lanes].T[lanes - edge :, :]

    def banded(field, weight, start, size):
        total = weight[start : start + size, 0:1] * field[start : start + size, :]
        for d in range(1, count + 1):
            col = edge + d - 1
            total = total + weight[start : start + size, col : col + 1] * field[start + d : start + d + size, :]
            total = total + weight[start - d : start - d + size, col : col + 1] * field[start - d : start - d + size, :]
        return total

    step = 16
    for start in range(edge, frame - edge, step):
        applied_f[start - edge : start - edge + step, :] = banded(slope_f, weight_f, start, step)
    out_curve[...] = product(slope_f[edge : frame - edge, :], applied_f[...])

    window = half + 2 * pad
    base = pl.multiple_of(h * half, edge)
    line = lax.broadcasted_iota(jnp.int32, (window, width), 0)
    weight_w[...] = weight_f[pl.ds(base, window), :]
    keep = (line >= jnp.where(even, pad, 0)) & (line < jnp.where(even, pad + half, window))
    for field, held in ((own_f, own_w), (near_f, near_w), (slope_f, slope_w)):
        held[...] = jnp.where(keep, field[pl.ds(base, window), :], 0.0)
    size = half + 2 * edge
    step = 16
    for held, out in ((own_w, out_own), (near_w, out_near), (slope_w, out_slope)):
        for start in range(0, size, step):
            line = lax.broadcasted_iota(jnp.int32, (step, width), 0) + start
            inside = (line >= jnp.where(even, 0, edge)) & (line < jnp.where(even, size, edge + half))
            out[start : start + step, :] = jnp.where(inside, banded(held, weight_w, start + edge, step), 0.0)


def multiply(visitor, visitor_rim, visitor_sum, ends, slope_applied, own_applied, near_applied, curve,
             out_keep, out_send, seen, moved):
    y, h, basis = place()
    even = h == 0
    core = lax.rem(basis, 2)
    rows = ends.shape[1]
    half = rows // 2
    size = half + edge
    at_near = (even & (y == 0)) | ((h == 1) & (y == 3))
    at = pl.multiple_of(jnp.where(even, edge, 0), edge)
    visitor_sign = sign_of(visitor_sum[0:1, :])
    seen[0:edge, :] = visitor_rim[0:edge, :] * visitor_sign
    seen[size:, :] = visitor_rim[0:edge, :] * visitor_sign
    seen[pl.ds(at, size), :] = visitor[...] * visitor_sign
    moved[...] = seen[...]

    @pl.when(at_near)
    def _():
        moved[0:edge, :] = moved[0:edge, :] - visitor_rim[edge : 2 * edge, :]
        beside = ends[h, pl.ds(pl.multiple_of(h * (half - edge), edge), size), :]
        moved[pl.ds(at, size), :] = seen[pl.ds(at, size), :] - beside

    scale = 1.0 / (2.0 * radial_step)
    cross = product(seen[...], slope_applied[...])
    first = product(own_applied[...], moved[...] * scale)
    second = product(near_applied[...], seen[...] * scale)
    low = core == 0
    for index, part in enumerate((cross, curve[...], first, second)):
        part = part.reshape(32, 2 * 4, part.shape[1])
        front, back = part[:, :4, :], part[:, 4:, :]
        out_keep[:, 4 * index : 4 * index + 4, :] = jnp.where(low, front, back)
        out_send[:, 4 * index : 4 * index + 4, :] = jnp.where(low, back, front)


def kernel(body, shapes, scratch, work, *operands, in_specs=None):
    extra = {} if in_specs is None else {"in_specs": in_specs}
    return pl.pallas_call(
        body,
        out_shape=[jax.ShapeDtypeStruct(shape, jnp.float32) for shape in shapes],
        scratch_shapes=[pltpu.VMEM(shape, jnp.float32) for shape in scratch],
        compiler_params=pltpu.CompilerParams(vmem_limit_bytes=40 * 1024 * 1024),
        cost_estimate=pl.CostEstimate(flops=work, bytes_accessed=4 * 1024 * 1024, transcendentals=0),
        **extra,
    )(*operands)


def shards(panels, end_panels, correlation_diag, correlation_band, band_reach, sign_rows):
    own = panels[0]
    rows, width = own.shape
    half = rows // 2
    rho, basis = lax.axis_index("rho"), lax.axis_index("basis")
    h, quarter = rho % 2, basis // 8 % 2
    reach = band_reach[None, :]

    half_rows, rim, visitor_rim, picked = kernel(
        prepare,
        [(half + edge, width), (3 * edge, width), (2 * edge, width), (32, edge, width)],
        [],
        1000000,
        own,
        end_panels[:, :edge],
        end_panels[:, rows - edge :],
        correlation_band,
        reach,
        sign_rows,
    )
    visitor = move(half_rows, swap_parity)
    picked = spread(picked, cube_groups).sum(0)
    near = move(own, to_neighbour)
    own_rim = move(rim, halo_own)
    near_rim = move(rim, halo_neighbour)
    visitor_rim = move(visitor_rim, halo_visitor)
    own_sum = picked + move(picked, swap_quarter)
    near_sum = move(own_sum, to_neighbour)
    visitor_sum = move(own_sum, swap_both)

    window = half + 4 * edge
    frame = rows + 4 * edge
    slope_applied, own_applied, near_applied, curve = kernel(
        apply,
        [(half + 2 * edge, width)] * 3 + [(width, width)],
        [(frame, width)] * 3
        + [(frame, 2 * edge), (2 * edge, rows), (frame - 2 * edge, width)]
        + [(window, width)] * 3
        + [(window, 2 * edge)],
        1000000000,
        own, near, end_panels, own_rim, near_rim, own_sum, near_sum, correlation_diag[None, :], correlation_band, reach,
    )
    keep, send = kernel(
        multiply,
        [(32, 16, width)] * 2,
        [(half + 2 * edge, width)] * 2,
        1000000000,
        visitor, visitor_rim, visitor_sum, end_panels, slope_applied, own_applied, near_applied, curve,
    )
    mine = keep + move(send, swap_core)
    mine = spread(mine.reshape(4, 8, 16, width), x_groups).sum(0)
    mine = spread(mine.reshape(2, 4, 16, width).transpose(1, 0, 2, 3), z_groups).sum(0)
    here = quarter == 0
    low, high = mine[0], mine[1]
    stay = jnp.where(here, low, high)
    go = jnp.where(here, high, low)
    mine = jnp.concatenate([go[:8], stay[8:]]) + move(jnp.concatenate([stay[:8], go[8:]]), swap_quarter)
    away = move(mine[:8], swap_both)
    second = move(mine[8:], from_neighbour)[4:]
    turn = jnp.where(h == 0, 1.0, -1.0)
    drift = turn * (mine[8:12] - second) + away[:4]
    return jnp.stack([drift, away[4:]], axis=1)[:, None]


def solution(mesh):
    in_specs = (
        P("rho", "basis", None),
        P(None, "basis", None),
        P("basis"),
        P(None, "basis"),
        P("basis"),
        P("rho", None),
    )
    out_specs = P("basis", "rho", None, None)
    return jax.shard_map(shards, mesh=mesh, in_specs=in_specs, out_specs=out_specs, check_vma=False)
```

```python
import jax
import jax.numpy as jnp
from jax import lax
from jax.experimental import pallas as pl
from jax.experimental.pallas import tpu as pltpu
from jax.sharding import PartitionSpec as P

radial_step = 0.5
edge = 8
both = ("rho", "basis")
exact = lax.Precision.HIGHEST


def hops(target):
    pairs = []
    for rho in range(8):
        for basis in range(64):
            to = target(rho // 2, rho % 2, basis // 16, basis // 2 % 8, basis % 2)
            if to is not None:
                y, h, x, z, core = to
                pairs.append((rho * 64 + basis, (y * 2 + h) * 64 + x * 16 + z * 2 + core))
    return pairs


def basis_step(x, z, core, by):
    index = x * 16 + z * 2 + core + by
    return (index // 16, index // 2 % 8, index % 2) if 0 <= index < 64 else None


def move(array, target):
    return lax.ppermute(array, both, hops(target))


def ring(xs, zs, cores):
    return [x * 16 + z * 2 + core for x in xs for z in zs for core in cores]


x_groups = [ring(range(4), (z,), (core,)) for z in range(8) for core in range(2)]
z_groups = [ring((x,), range(8), (core,)) for x in range(4) for core in range(2)]
plane_groups = [ring(range(4), (z,), range(2)) for z in range(8)]


def spread(array, groups):
    return lax.all_to_all(array, "basis", 0, 0, axis_index_groups=groups)


def gather_sum(array, groups):
    count = len(groups[0])
    return spread(jnp.broadcast_to(array[None], (count, *array.shape)), groups).sum(0)


def swap_core(y, h, x, z, core):
    return y, h, x, z, 1 - core


def swap_parity(y, h, x, z, core):
    return y, 1 - h, x, z, core


def to_neighbour(y, h, x, z, core):
    return ((y - 1) if h == 0 else (y + 1)) % 4, h, x, z, core


def from_neighbour(y, h, x, z, core):
    return ((y + 1) if h == 0 else (y - 1)) % 4, h, x, z, core


def halo_own(y, h, x, z, core):
    to = basis_step(x, z, core, 1 if h == 0 else -1)
    return None if to is None else (y, h, *to)


def halo_visitor(y, h, x, z, core):
    to = basis_step(x, z, core, -1 if h == 0 else 1)
    return None if to is None else (y, 1 - h, *to)


def product(a, b):
    return lax.dot_general(
        a, b, (((0,), (0,)), ((), ())), precision=exact, preferred_element_type=jnp.float32
    )


def sign_of(values):
    return jnp.where(values > 0.0, 1.0, jnp.where(values < 0.0, -1.0, 0.0))


def place():
    rho, basis = lax.axis_index("rho"), lax.axis_index("basis")
    return lax.div(rho, 2), lax.rem(rho, 2), basis


def prepare(own, ends_first, ends_last, band, reach, rows_of, out_half, out_rim, out_visitor, out_picked):
    y, h, basis = place()
    rows, width = own.shape
    half = rows // 2
    out_half[...] = own[pl.ds(pl.multiple_of((1 - h) * (half - edge), edge), half + edge), :]
    spot = rows_of[...] - basis * rows
    step = 64
    picked = jnp.zeros((edge, width), jnp.float32)
    for start in range(0, rows, step):
        line = lax.broadcasted_iota(jnp.int32, (step, width), 0) + start
        hit = jnp.where(line == spot, own[start : start + step, :], 0.0)
        picked = picked + hit.reshape(step // edge, edge, width).sum(0)
    picked = jnp.broadcast_to(picked.sum(0, keepdims=True), (edge, width))
    out_picked[...] = jnp.broadcast_to(picked[None], out_picked.shape)
    even = h == 0
    depth = lax.broadcasted_iota(jnp.int32, band.shape, 0) + 1
    masked = jnp.where(depth <= reach[...].reshape(1, rows), band[...], 0.0)
    out_rim[0:edge, :] = jnp.where(even, own[rows - edge :, :], own[:edge, :])
    out_rim[edge : 2 * edge, :] = jnp.zeros((edge, width), jnp.float32)
    out_rim[edge : edge + band.shape[0], :] = masked[:, rows - width :]
    out_rim[2 * edge :, :] = jnp.where(even, ends_last[1], ends_first[0])
    out_visitor[0:edge, :] = own[rows - edge :, :]
    out_visitor[edge:, :] = ends_last[0]


def apply(own, near, ends, own_rim, near_rim, own_sum, diag, band, reach,
          out_slope, out_own, out_near, out_curve, own_f, near_f, slope_f, weight_f, turned, applied_f, own_w, near_w, slope_w, weight_w):
    y, h, basis = place()
    rows, width = own.shape
    half = rows // 2
    pad = 2 * edge
    frame = rows + 2 * pad
    even = h == 0
    at_far = (even & (y == 3)) | ((h == 1) & (y == 0))
    far = 1 - h
    own_sign = sign_of(own_sum[0:1, :])
    near_sign = sign_of(near_rim[edge : edge + 1, :])
    has_low = (even & (basis > 0)).astype(jnp.float32)
    has_high = ((h == 1) & (basis < 63)).astype(jnp.float32)
    blank = jnp.zeros((pad, width), jnp.float32)
    for field in (own_f, near_f):
        field[0:pad, :] = blank
        field[pad + rows :, :] = blank
    own_f[pad : pad + rows, :] = own[...] * own_sign
    own_f[edge:pad, :] = own_rim[0:edge, :] * own_sign * has_low
    own_f[pad + rows : pad + rows + edge, :] = own_rim[0:edge, :] * own_sign * has_high

    @pl.when(at_far)
    def _():
        near_f[pad : pad + rows, :] = ends[far]
        near_f[edge:pad, :] = own_rim[2 * edge :, :] * has_low
        near_f[pad + rows : pad + rows + edge, :] = own_rim[2 * edge :, :] * has_high

    def fill_near():
        near_f[pad : pad + rows, :] = near[...] * near_sign
        near_f[edge:pad, :] = near_rim[0:edge, :] * near_sign * has_low
        near_f[pad + rows : pad + rows + edge, :] = near_rim[0:edge, :] * near_sign * has_high

    pl.when(jnp.logical_not(at_far))(fill_near)
    turn = jnp.where(even, 1.0, -1.0)
    slope_f[...] = (near_f[...] - own_f[...]) * turn / (2.0 * radial_step)
    pl.when(at_far)(fill_near)

    count = band.shape[0]
    depth = lax.broadcasted_iota(jnp.int32, band.shape, 0) + 1
    masked = jnp.where(depth <= reach[...], band[...], 0.0)
    lanes = 128
    turned[...] = jnp.zeros(turned.shape, jnp.float32)
    turned[0:1, :] = diag[...]
    turned[edge : edge + count, :] = masked
    weight_f[...] = jnp.zeros(weight_f.shape, jnp.float32)
    for start in range(0, rows, lanes):
        weight_f[pad + start : pad + start + lanes, :] = turned[:, start : start + lanes].T
    before = own_rim[edge : 2 * edge, width - lanes :]
    lane = lax.broadcasted_iota(jnp.int32, before.shape, 1)
    level = lax.broadcasted_iota(jnp.int32, before.shape, 0) + 1
    before = jnp.where(lane + level >= lanes, before, 0.0) * has_low
    turned[edge : 2 * edge, 0:lanes] = before
    turned[0:edge, 0:lanes] = jnp.zeros((edge, lanes), jnp.float32)
    weight_f[edge:pad, :] = turned[:, 0:lanes].T[lanes - edge :, :]

    def banded(field, weight, start, size):
        total = weight[start : start + size, 0:1] * field[start : start + size, :]
        for d in range(1, count + 1):
            col = edge + d - 1
            total = total + weight[start : start + size, col : col + 1] * field[start + d : start + d + size, :]
            total = total + weight[start - d : start - d + size, col : col + 1] * field[start - d : start - d + size, :]
        return total

    step = 16
    for start in range(edge, frame - edge, step):
        applied_f[start - edge : start - edge + step, :] = banded(slope_f, weight_f, start, step)
    out_curve[...] = product(slope_f[edge : frame - edge, :], applied_f[...])

    window = half + 2 * pad
    base = pl.multiple_of(h * half, edge)
    line = lax.broadcasted_iota(jnp.int32, (window, width), 0)
    weight_w[...] = weight_f[pl.ds(base, window), :]
    keep = (line >= jnp.where(even, pad, 0)) & (line < jnp.where(even, pad + half, window))
    for field, held in ((own_f, own_w), (near_f, near_w), (slope_f, slope_w)):
        held[...] = jnp.where(keep, field[pl.ds(base, window), :], 0.0)
    size = half + 2 * edge
    step = 16
    for held, out in ((own_w, out_own), (near_w, out_near), (slope_w, out_slope)):
        for start in range(0, size, step):
            line = lax.broadcasted_iota(jnp.int32, (step, width), 0) + start
            inside = (line >= jnp.where(even, 0, edge)) & (line < jnp.where(even, size, edge + half))
            out[start : start + step, :] = jnp.where(inside, banded(held, weight_w, start + edge, step), 0.0)


def multiply(visitor, visitor_rim, ends, slope_applied, own_applied, near_applied, curve,
             out_keep, out_send, seen, moved):
    y, h, basis = place()
    even = h == 0
    core = lax.rem(basis, 2)
    rows = ends.shape[1]
    half = rows // 2
    size = half + edge
    at_far = (even & (y == 3)) | ((h == 1) & (y == 0))
    at = pl.multiple_of(jnp.where(even, edge, 0), edge)
    seen[0:edge, :] = visitor_rim[0:edge, :]
    seen[size:, :] = visitor_rim[0:edge, :]
    seen[pl.ds(at, size), :] = visitor[...]
    moved[...] = seen[...]

    @pl.when(at_far)
    def _():
        moved[0:edge, :] = visitor_rim[edge : 2 * edge, :]
        moved[pl.ds(at, size), :] = ends[h, pl.ds(pl.multiple_of(h * (half - edge), edge), size), :]

    scale = 1.0 / (2.0 * radial_step)
    cross = product(seen[...], slope_applied[...])
    first = product(own_applied[...], seen[...] * scale)
    second = product(near_applied[...], moved[...] * scale)
    low = core == 0
    for index, part in enumerate((cross, curve[...], first, second)):
        part = part.reshape(32, 2 * 4, part.shape[1])
        front, back = part[:, :4, :], part[:, 4:, :]
        out_keep[:, 4 * index : 4 * index + 4, :] = jnp.where(low, front, back)
        out_send[:, 4 * index : 4 * index + 4, :] = jnp.where(low, back, front)


def kernel(body, shapes, scratch, work, *operands):
    return pl.pallas_call(
        body,
        out_shape=[jax.ShapeDtypeStruct(shape, jnp.float32) for shape in shapes],
        scratch_shapes=[pltpu.VMEM(shape, jnp.float32) for shape in scratch],
        compiler_params=pltpu.CompilerParams(vmem_limit_bytes=40 * 1024 * 1024),
        cost_estimate=pl.CostEstimate(flops=work, bytes_accessed=4 * 1024 * 1024, transcendentals=0),
    )(*operands)


def whole(shape):
    return pl.BlockSpec(shape, lambda i: (0,) * len(shape))


def shards(panels, end_panels, correlation_diag, correlation_band, band_reach, sign_rows):
    own = panels[0]
    rows, width = own.shape
    half = rows // 2
    h = lax.axis_index("rho") % 2
    reach = band_reach[None, :]

    half_rows, rim, visitor_rim, picked = pl.pallas_call(
        prepare,
        grid=(1,),
        in_specs=[
            whole(own.shape),
            whole((2, edge, width)),
            pl.BlockSpec((2, edge, width), lambda i: (0, rows // edge - 1, 0)),
            whole(correlation_band.shape),
            whole(band_reach.shape),
            whole(sign_rows.shape),
        ],
        out_specs=[whole((half + edge, width)), whole((3 * edge, width)), whole((2 * edge, width)), whole((8, edge, width))],
        out_shape=[
            jax.ShapeDtypeStruct(shape, jnp.float32)
            for shape in ((half + edge, width), (3 * edge, width), (2 * edge, width), (8, edge, width))
        ],
        compiler_params=pltpu.CompilerParams(vmem_limit_bytes=60 * 1024 * 1024),
        cost_estimate=pl.CostEstimate(flops=1000000, bytes_accessed=2 * 1024 * 1024, transcendentals=0),
    )(own, end_panels, end_panels, correlation_band, band_reach, sign_rows)
    own_rim = move(rim, halo_own)
    picked = spread(picked, z_groups).sum(0)
    half_rows, picked, own_rim, visitor_rim, own = lax.optimization_barrier(
        (half_rows, picked, own_rim, visitor_rim, own)
    )
    visitor = move(half_rows, swap_parity)
    visitor_rim = move(visitor_rim, halo_visitor)
    near = move(own, to_neighbour)
    own_sum = gather_sum(picked, plane_groups)
    near_rim = move(jnp.concatenate([own_rim[:edge], own_sum]), to_neighbour)

    window = half + 4 * edge
    frame = rows + 4 * edge
    slope_applied, own_applied, near_applied, curve = kernel(
        apply,
        [(half + 2 * edge, width)] * 3 + [(width, width)],
        [(frame, width)] * 3
        + [(frame, 2 * edge), (2 * edge, rows), (frame - 2 * edge, width)]
        + [(window, width)] * 3
        + [(window, 2 * edge)],
        1000000000,
        own, near, end_panels, own_rim, near_rim, own_sum, correlation_diag[None, :], correlation_band, reach,
    )
    keep, send = kernel(
        multiply,
        [(32, 16, width)] * 2,
        [(half + 2 * edge, width)] * 2,
        1000000000,
        visitor, visitor_rim, end_panels, slope_applied, own_applied, near_applied, curve,
    )
    mine = keep + move(send, swap_core)
    mine = spread(mine.reshape(4, 8, 16, width), x_groups).sum(0)
    mine = spread(mine, z_groups).sum(0)
    y, basis = lax.axis_index("rho") // 2, lax.axis_index("basis")
    at_far = jnp.where(h == 0, y == 3, y == 0)
    line = jnp.arange(edge)[:, None]
    signs = jnp.where(line == 0, jnp.sign(own_sum), jnp.where(at_far, 1.0, jnp.sign(near_rim[edge:])))
    away = move(jnp.concatenate([mine[:8], signs]), swap_parity)
    second = move(mine[8:], from_neighbour)[4:]
    turn = jnp.where(h == 0, 1.0, -1.0)
    here = lax.dynamic_slice_in_dim(signs[0], basis * 4, 4)[:, None]
    drift = turn * (mine[8:12] * away[8] - second * away[9]) + here * away[:4]
    return jnp.stack([drift, away[4:8]], axis=1)[:, None]


def solution(mesh):
    in_specs = (
        P("rho", "basis", None),
        P(None, "basis", None),
        P("basis"),
        P(None, "basis"),
        P("basis"),
        P("rho", None),
    )
    out_specs = P("basis", "rho", None, None)
    return jax.shard_map(shards, mesh=mesh, in_specs=in_specs, out_specs=out_specs, check_vma=False)
```

```python
import jax
import jax.numpy as jnp
from jax import lax
from jax.experimental import pallas as pl
from jax.experimental.pallas import tpu as pltpu
from jax.sharding import PartitionSpec as P

radial_step = 0.5
edge = 8
both = ("rho", "basis")
exact = lax.Precision.HIGHEST


def hops(target):
    pairs = []
    for rho in range(8):
        for basis in range(64):
            to = target(rho // 2, rho % 2, basis // 16, basis // 2 % 8, basis % 2)
            if to is not None:
                y, h, x, z, core = to
                pairs.append((rho * 64 + basis, (y * 2 + h) * 64 + x * 16 + z * 2 + core))
    return pairs


def basis_step(x, z, core, by):
    index = x * 16 + z * 2 + core + by
    return (index // 16, index // 2 % 8, index % 2) if 0 <= index < 64 else None


def move(array, target):
    return lax.ppermute(array, both, hops(target))


def ring(xs, zs, cores):
    return [x * 16 + z * 2 + core for x in xs for z in zs for core in cores]


x_groups = [ring(range(4), (z,), (core,)) for z in range(8) for core in range(2)]
z_groups = [ring((x,), range(8), (core,)) for x in range(4) for core in range(2)]
plane_groups = [ring(range(4), (z,), range(2)) for z in range(8)]


def spread(array, groups):
    return lax.all_to_all(array, "basis", 0, 0, axis_index_groups=groups)


def gather_sum(array, groups):
    count = len(groups[0])
    return spread(jnp.broadcast_to(array[None], (count, *array.shape)), groups).sum(0)


def swap_core(y, h, x, z, core):
    return y, h, x, z, 1 - core


def swap_parity(y, h, x, z, core):
    return y, 1 - h, x, z, core


def to_neighbour(y, h, x, z, core):
    return ((y - 1) if h == 0 else (y + 1)) % 4, h, x, z, core


def from_neighbour(y, h, x, z, core):
    return ((y + 1) if h == 0 else (y - 1)) % 4, h, x, z, core


def halo_own(y, h, x, z, core):
    to = basis_step(x, z, core, 1 if h == 0 else -1)
    return None if to is None else (y, h, *to)


def halo_visitor(y, h, x, z, core):
    to = basis_step(x, z, core, -1 if h == 0 else 1)
    return None if to is None else (y, 1 - h, *to)


def product(a, b):
    return lax.dot_general(
        a, b, (((0,), (0,)), ((), ())), precision=exact, preferred_element_type=jnp.float32
    )


def sign_of(values):
    return jnp.where(values > 0.0, 1.0, jnp.where(values < 0.0, -1.0, 0.0))


def place():
    rho, basis = lax.axis_index("rho"), lax.axis_index("basis")
    return lax.div(rho, 2), lax.rem(rho, 2), basis


def prepare(own, ends_first, ends_last, band, reach, rows_of, out_half, out_rim, out_visitor, out_picked):
    y, h, basis = place()
    rows, width = own.shape
    half = rows // 2
    out_half[...] = own[pl.ds(pl.multiple_of((1 - h) * (half - edge), edge), half + edge), :]
    spot = rows_of[...] - basis * rows
    step = 64
    picked = jnp.zeros((edge, width), jnp.float32)
    for start in range(0, rows, step):
        line = lax.broadcasted_iota(jnp.int32, (step, width), 0) + start
        hit = jnp.where(line == spot, own[start : start + step, :], 0.0)
        picked = picked + hit.reshape(step // edge, edge, width).sum(0)
    picked = picked.sum(0, keepdims=True)
    out_picked[...] = jnp.broadcast_to(picked[None], out_picked.shape)
    even = h == 0
    depth = lax.broadcasted_iota(jnp.int32, band.shape, 0) + 1
    masked = jnp.where(depth <= reach[...].reshape(1, rows), band[...], 0.0)
    out_rim[0:edge, :] = jnp.where(even, own[rows - edge :, :], own[:edge, :])
    out_rim[edge : 2 * edge, :] = jnp.zeros((edge, width), jnp.float32)
    out_rim[edge : edge + band.shape[0], :] = masked[:, rows - width :]
    out_rim[2 * edge :, :] = jnp.where(even, ends_last[1], ends_first[0])
    out_visitor[0:edge, :] = own[rows - edge :, :]
    out_visitor[edge:, :] = ends_last[0]


def apply(own, near, ends, own_rim, near_rim, own_sum, diag, band, reach,
          out_slope, out_own, out_near, out_curve, own_f, near_f, slope_f, weight_f, turned, applied_f, own_w, near_w, slope_w, weight_w):
    y, h, basis = place()
    rows, width = own.shape
    half = rows // 2
    pad = 2 * edge
    frame = rows + 2 * pad
    even = h == 0
    at_far = (even & (y == 3)) | ((h == 1) & (y == 0))
    far = 1 - h
    own_sign = sign_of(own_sum[0:1, :])
    near_sign = sign_of(near_rim[edge : edge + 1, :])
    has_low = (even & (basis > 0)).astype(jnp.float32)
    has_high = ((h == 1) & (basis < 63)).astype(jnp.float32)
    blank = jnp.zeros((pad, width), jnp.float32)
    for field in (own_f, near_f):
        field[0:pad, :] = blank
        field[pad + rows :, :] = blank
    own_f[pad : pad + rows, :] = own[...] * own_sign
    own_f[edge:pad, :] = own_rim[0:edge, :] * own_sign * has_low
    own_f[pad + rows : pad + rows + edge, :] = own_rim[0:edge, :] * own_sign * has_high

    @pl.when(at_far)
    def _():
        near_f[pad : pad + rows, :] = ends[far]
        near_f[edge:pad, :] = own_rim[2 * edge :, :] * has_low
        near_f[pad + rows : pad + rows + edge, :] = own_rim[2 * edge :, :] * has_high

    def fill_near():
        near_f[pad : pad + rows, :] = near[...] * near_sign
        near_f[edge:pad, :] = near_rim[0:edge, :] * near_sign * has_low
        near_f[pad + rows : pad + rows + edge, :] = near_rim[0:edge, :] * near_sign * has_high

    pl.when(jnp.logical_not(at_far))(fill_near)
    turn = jnp.where(even, 1.0, -1.0)
    slope_f[...] = (near_f[...] - own_f[...]) * turn / (2.0 * radial_step)
    pl.when(at_far)(fill_near)

    count = band.shape[0]
    depth = lax.broadcasted_iota(jnp.int32, band.shape, 0) + 1
    masked = jnp.where(depth <= reach[...], band[...], 0.0)
    lanes = 128
    turned[...] = jnp.zeros(turned.shape, jnp.float32)
    turned[0:1, :] = diag[...]
    turned[edge : edge + count, :] = masked
    weight_f[...] = jnp.zeros(weight_f.shape, jnp.float32)
    for start in range(0, rows, lanes):
        weight_f[pad + start : pad + start + lanes, :] = turned[:, start : start + lanes].T
    before = own_rim[edge : 2 * edge, width - lanes :]
    lane = lax.broadcasted_iota(jnp.int32, before.shape, 1)
    level = lax.broadcasted_iota(jnp.int32, before.shape, 0) + 1
    before = jnp.where(lane + level >= lanes, before, 0.0) * has_low
    turned[edge : 2 * edge, 0:lanes] = before
    turned[0:edge, 0:lanes] = jnp.zeros((edge, lanes), jnp.float32)
    weight_f[edge:pad, :] = turned[:, 0:lanes].T[lanes - edge :, :]

    def banded(field, weight, start, size):
        total = weight[start : start + size, 0:1] * field[start : start + size, :]
        for d in range(1, count + 1):
            col = edge + d - 1
            total = total + weight[start : start + size, col : col + 1] * field[start + d : start + d + size, :]
            total = total + weight[start - d : start - d + size, col : col + 1] * field[start - d : start - d + size, :]
        return total

    step = 16
    for start in range(edge, frame - edge, step):
        applied_f[start - edge : start - edge + step, :] = banded(slope_f, weight_f, start, step)
    out_curve[...] = product(slope_f[edge : frame - edge, :], applied_f[...])

    window = half + 2 * pad
    base = pl.multiple_of(h * half, edge)
    line = lax.broadcasted_iota(jnp.int32, (window, width), 0)
    weight_w[...] = weight_f[pl.ds(base, window), :]
    keep = (line >= jnp.where(even, pad, 0)) & (line < jnp.where(even, pad + half, window))
    for field, held in ((own_f, own_w), (near_f, near_w), (slope_f, slope_w)):
        held[...] = jnp.where(keep, field[pl.ds(base, window), :], 0.0)
    size = half + 2 * edge
    step = 16
    for held, out in ((own_w, out_own), (near_w, out_near), (slope_w, out_slope)):
        for start in range(0, size, step):
            line = lax.broadcasted_iota(jnp.int32, (step, width), 0) + start
            inside = (line >= jnp.where(even, 0, edge)) & (line < jnp.where(even, size, edge + half))
            out[start : start + step, :] = jnp.where(inside, banded(held, weight_w, start + edge, step), 0.0)


def multiply(visitor, visitor_rim, ends, slope_applied, own_applied, near_applied, curve,
             out_keep, out_send, seen, moved):
    y, h, basis = place()
    even = h == 0
    core = lax.rem(basis, 2)
    rows = ends.shape[1]
    half = rows // 2
    size = half + edge
    at_far = (even & (y == 3)) | ((h == 1) & (y == 0))
    at = pl.multiple_of(jnp.where(even, edge, 0), edge)
    seen[0:edge, :] = visitor_rim[0:edge, :]
    seen[size:, :] = visitor_rim[0:edge, :]
    seen[pl.ds(at, size), :] = visitor[...]
    moved[...] = seen[...]

    @pl.when(at_far)
    def _():
        moved[0:edge, :] = visitor_rim[edge : 2 * edge, :]
        moved[pl.ds(at, size), :] = ends[h, pl.ds(pl.multiple_of(h * (half - edge), edge), size), :]

    scale = 1.0 / (2.0 * radial_step)
    cross = product(seen[...], slope_applied[...])
    first = product(own_applied[...], seen[...] * scale)
    second = product(near_applied[...], moved[...] * scale)
    low = core == 0
    for index, part in enumerate((cross, curve[...], first, second)):
        part = part.reshape(32, 2 * 4, part.shape[1])
        front, back = part[:, :4, :], part[:, 4:, :]
        out_keep[:, 4 * index : 4 * index + 4, :] = jnp.where(low, front, back)
        out_send[:, 4 * index : 4 * index + 4, :] = jnp.where(low, back, front)


def kernel(body, shapes, scratch, work, *operands):
    return pl.pallas_call(
        body,
        out_shape=[jax.ShapeDtypeStruct(shape, jnp.float32) for shape in shapes],
        scratch_shapes=[pltpu.VMEM(shape, jnp.float32) for shape in scratch],
        compiler_params=pltpu.CompilerParams(vmem_limit_bytes=40 * 1024 * 1024),
        cost_estimate=pl.CostEstimate(flops=work, bytes_accessed=4 * 1024 * 1024, transcendentals=0),
    )(*operands)


def whole(shape):
    return pl.BlockSpec(shape, lambda i: (0,) * len(shape))


def shards(panels, end_panels, correlation_diag, correlation_band, band_reach, sign_rows):
    own = panels[0]
    rows, width = own.shape
    half = rows // 2
    h = lax.axis_index("rho") % 2
    reach = band_reach[None, :]

    half_rows, rim, visitor_rim, picked = pl.pallas_call(
        prepare,
        grid=(1,),
        in_specs=[
            whole(own.shape),
            whole((2, edge, width)),
            pl.BlockSpec((2, edge, width), lambda i: (0, rows // edge - 1, 0)),
            whole(correlation_band.shape),
            whole(band_reach.shape),
            whole(sign_rows.shape),
        ],
        out_specs=[whole((half + edge, width)), whole((3 * edge, width)), whole((2 * edge, width)), whole((8, 1, width))],
        out_shape=[
            jax.ShapeDtypeStruct(shape, jnp.float32)
            for shape in ((half + edge, width), (3 * edge, width), (2 * edge, width), (8, 1, width))
        ],
        compiler_params=pltpu.CompilerParams(vmem_limit_bytes=60 * 1024 * 1024),
        cost_estimate=pl.CostEstimate(flops=1000000, bytes_accessed=2 * 1024 * 1024, transcendentals=0),
    )(own, end_panels, end_panels, correlation_band, band_reach, sign_rows)
    own_rim = move(rim, halo_own)
    picked = spread(picked, z_groups).sum(0)
    near = move(own, to_neighbour)
    half_rows, picked, own_rim, visitor_rim = lax.optimization_barrier((half_rows, picked, own_rim, visitor_rim))
    visitor = move(half_rows, swap_parity)
    visitor_rim = move(visitor_rim, halo_visitor)
    own_sum = gather_sum(picked, plane_groups)
    near_rim = move(jnp.concatenate([own_rim[:edge], jnp.broadcast_to(own_sum, (edge, width))]), to_neighbour)

    window = half + 4 * edge
    frame = rows + 4 * edge
    slope_applied, own_applied, near_applied, curve = kernel(
        apply,
        [(half + 2 * edge, width)] * 3 + [(width, width)],
        [(frame, width)] * 3
        + [(frame, 2 * edge), (2 * edge, rows), (frame - 2 * edge, width)]
        + [(window, width)] * 3
        + [(window, 2 * edge)],
        1000000000,
        own, near, end_panels, own_rim, near_rim, own_sum, correlation_diag[None, :], correlation_band, reach,
    )
    keep, send = kernel(
        multiply,
        [(32, 16, width)] * 2,
        [(half + 2 * edge, width)] * 2,
        1000000000,
        visitor, visitor_rim, end_panels, slope_applied, own_applied, near_applied, curve,
    )
    mine = keep + move(send, swap_core)
    mine = spread(mine.reshape(4, 8, 16, width), x_groups).sum(0)
    mine = spread(mine, z_groups).sum(0)
    y, basis = lax.axis_index("rho") // 2, lax.axis_index("basis")
    at_far = jnp.where(h == 0, y == 3, y == 0)
    line = jnp.arange(edge)[:, None]
    signs = jnp.where(line == 0, jnp.sign(own_sum), jnp.where(at_far, 1.0, jnp.sign(near_rim[edge:])))
    away = move(jnp.concatenate([mine[:8], signs]), swap_parity)
    second = move(mine[8:], from_neighbour)[4:]
    turn = jnp.where(h == 0, 1.0, -1.0)
    here = lax.dynamic_slice_in_dim(signs[0], basis * 4, 4)[:, None]
    drift = turn * (mine[8:12] * away[8] - second * away[9]) + here * away[:4]
    return jnp.stack([drift, away[4:8]], axis=1)[:, None]


def solution(mesh):
    in_specs = (
        P("rho", "basis", None),
        P(None, "basis", None),
        P("basis"),
        P(None, "basis"),
        P("basis"),
        P("rho", None),
    )
    out_specs = P("basis", "rho", None, None)
    return jax.shard_map(shards, mesh=mesh, in_specs=in_specs, out_specs=out_specs, check_vma=False)
```

```python
import jax
import jax.numpy as jnp
from jax import lax
from jax.experimental import pallas as pl
from jax.experimental.pallas import tpu as pltpu
from jax.sharding import PartitionSpec as P

radial_step = 0.5
edge = 8
both = ("rho", "basis")
exact = lax.Precision.HIGHEST


def hops(target):
    pairs = []
    for rho in range(8):
        for basis in range(64):
            to = target(rho // 2, rho % 2, basis // 16, basis // 2 % 8, basis % 2)
            if to is not None:
                y, h, x, z, core = to
                pairs.append((rho * 64 + basis, (y * 2 + h) * 64 + x * 16 + z * 2 + core))
    return pairs


def basis_step(x, z, core, by):
    index = x * 16 + z * 2 + core + by
    return (index // 16, index // 2 % 8, index % 2) if 0 <= index < 64 else None


def move(array, target):
    return lax.ppermute(array, both, hops(target))


def ring(xs, zs, cores):
    return [x * 16 + z * 2 + core for x in xs for z in zs for core in cores]


x_groups = [ring(range(4), (z,), (core,)) for z in range(8) for core in range(2)]
z_groups = [ring((x,), range(8), (core,)) for x in range(4) for core in range(2)]
plane_groups = [ring(range(4), (z,), range(2)) for z in range(8)]


def spread(array, groups):
    return lax.all_to_all(array, "basis", 0, 0, axis_index_groups=groups)


def gather_sum(array, groups):
    count = len(groups[0])
    return spread(jnp.broadcast_to(array[None], (count, *array.shape)), groups).sum(0)


def swap_core(y, h, x, z, core):
    return y, h, x, z, 1 - core


def swap_parity(y, h, x, z, core):
    return y, 1 - h, x, z, core


def to_neighbour(y, h, x, z, core):
    return ((y - 1) if h == 0 else (y + 1)) % 4, h, x, z, core


def from_neighbour(y, h, x, z, core):
    return ((y + 1) if h == 0 else (y - 1)) % 4, h, x, z, core


def halo_own(y, h, x, z, core):
    to = basis_step(x, z, core, 1 if h == 0 else -1)
    return None if to is None else (y, h, *to)


def halo_visitor(y, h, x, z, core):
    to = basis_step(x, z, core, -1 if h == 0 else 1)
    return None if to is None else (y, 1 - h, *to)


def product(a, b):
    return lax.dot_general(
        a, b, (((0,), (0,)), ((), ())), precision=exact, preferred_element_type=jnp.float32
    )


def sign_of(values):
    return jnp.where(values > 0.0, 1.0, jnp.where(values < 0.0, -1.0, 0.0))


def halves(a):
    high = a.astype(jnp.bfloat16)
    return high, (a - high.astype(jnp.float32)).astype(jnp.bfloat16)


def product_of_halves(a, b):
    def dot(x, y):
        return lax.dot_general(x, y, (((0,), (0,)), ((), ())), preferred_element_type=jnp.float32)

    return dot(a[0], b[0]) + (dot(a[0], b[1]) + dot(a[1], b[0]))


def place():
    rho, basis = lax.axis_index("rho"), lax.axis_index("basis")
    return lax.div(rho, 2), lax.rem(rho, 2), basis


def prepare(own, ends_first, ends_last, band, reach, rows_of, out_half, out_rim, out_visitor, out_picked):
    y, h, basis = place()
    rows, width = own.shape
    half = rows // 2
    out_half[...] = own[pl.ds(pl.multiple_of((1 - h) * (half - edge), edge), half + edge), :]
    spot = rows_of[...] - basis * rows
    step = 64
    picked = jnp.zeros((edge, width), jnp.float32)
    for start in range(0, rows, step):
        line = lax.broadcasted_iota(jnp.int32, (step, width), 0) + start
        hit = jnp.where(line == spot, own[start : start + step, :], 0.0)
        picked = picked + hit.reshape(step // edge, edge, width).sum(0)
    picked = picked.sum(0, keepdims=True)
    out_picked[...] = jnp.broadcast_to(picked[None], out_picked.shape)
    even = h == 0
    depth = lax.broadcasted_iota(jnp.int32, band.shape, 0) + 1
    masked = jnp.where(depth <= reach[...].reshape(1, rows), band[...], 0.0)
    out_rim[0:edge, :] = jnp.where(even, own[rows - edge :, :], own[:edge, :])
    out_rim[edge : 2 * edge, :] = jnp.zeros((edge, width), jnp.float32)
    out_rim[edge : edge + band.shape[0], :] = masked[:, rows - width :]
    out_rim[2 * edge :, :] = jnp.where(even, ends_last[1], ends_first[0])
    out_visitor[0:edge, :] = own[rows - edge :, :]
    out_visitor[edge:, :] = ends_last[0]


def apply(own, near, ends, own_rim, near_rim, own_sum, diag, band, reach,
          out_slope, out_own, out_near, out_curve, own_f, near_f, slope_f, weight_f, turned, applied_f, own_w, near_w, slope_w, weight_w):
    y, h, basis = place()
    rows, width = own.shape
    half = rows // 2
    pad = 2 * edge
    frame = rows + 2 * pad
    even = h == 0
    at_far = (even & (y == 3)) | ((h == 1) & (y == 0))
    far = 1 - h
    own_sign = sign_of(own_sum[0:1, :])
    near_sign = sign_of(near_rim[edge : edge + 1, :])
    has_low = (even & (basis > 0)).astype(jnp.float32)
    has_high = ((h == 1) & (basis < 63)).astype(jnp.float32)
    blank = jnp.zeros((pad, width), jnp.float32)
    for field in (own_f, near_f):
        field[0:pad, :] = blank
        field[pad + rows :, :] = blank
    own_f[pad : pad + rows, :] = own[...] * own_sign
    own_f[edge:pad, :] = own_rim[0:edge, :] * own_sign * has_low
    own_f[pad + rows : pad + rows + edge, :] = own_rim[0:edge, :] * own_sign * has_high

    @pl.when(at_far)
    def _():
        near_f[pad : pad + rows, :] = ends[far]
        near_f[edge:pad, :] = own_rim[2 * edge :, :] * has_low
        near_f[pad + rows : pad + rows + edge, :] = own_rim[2 * edge :, :] * has_high

    def fill_near():
        near_f[pad : pad + rows, :] = near[...] * near_sign
        near_f[edge:pad, :] = near_rim[0:edge, :] * near_sign * has_low
        near_f[pad + rows : pad + rows + edge, :] = near_rim[0:edge, :] * near_sign * has_high

    pl.when(jnp.logical_not(at_far))(fill_near)
    turn = jnp.where(even, 1.0, -1.0)
    slope_f[...] = (near_f[...] - own_f[...]) * turn / (2.0 * radial_step)
    pl.when(at_far)(fill_near)

    count = band.shape[0]
    depth = lax.broadcasted_iota(jnp.int32, band.shape, 0) + 1
    masked = jnp.where(depth <= reach[...], band[...], 0.0)
    lanes = 128
    turned[...] = jnp.zeros(turned.shape, jnp.float32)
    turned[0:1, :] = diag[...]
    turned[edge : edge + count, :] = masked
    weight_f[...] = jnp.zeros(weight_f.shape, jnp.float32)
    for start in range(0, rows, lanes):
        weight_f[pad + start : pad + start + lanes, :] = turned[:, start : start + lanes].T
    before = own_rim[edge : 2 * edge, width - lanes :]
    lane = lax.broadcasted_iota(jnp.int32, before.shape, 1)
    level = lax.broadcasted_iota(jnp.int32, before.shape, 0) + 1
    before = jnp.where(lane + level >= lanes, before, 0.0) * has_low
    turned[edge : 2 * edge, 0:lanes] = before
    turned[0:edge, 0:lanes] = jnp.zeros((edge, lanes), jnp.float32)
    weight_f[edge:pad, :] = turned[:, 0:lanes].T[lanes - edge :, :]

    def banded(field, weight, start, size):
        total = weight[start : start + size, 0:1] * field[start : start + size, :]
        for d in range(1, count + 1):
            col = edge + d - 1
            total = total + weight[start : start + size, col : col + 1] * field[start + d : start + d + size, :]
            total = total + weight[start - d : start - d + size, col : col + 1] * field[start - d : start - d + size, :]
        return total

    step = 16
    for start in range(edge, frame - edge, step):
        applied_f[start - edge : start - edge + step, :] = banded(slope_f, weight_f, start, step)
    out_curve[...] = product(slope_f[edge : frame - edge, :], applied_f[...])

    window = half + 2 * pad
    base = pl.multiple_of(h * half, edge)
    line = lax.broadcasted_iota(jnp.int32, (window, width), 0)
    weight_w[...] = weight_f[pl.ds(base, window), :]
    keep = (line >= jnp.where(even, pad, 0)) & (line < jnp.where(even, pad + half, window))
    for field, held in ((own_f, own_w), (near_f, near_w), (slope_f, slope_w)):
        held[...] = jnp.where(keep, field[pl.ds(base, window), :], 0.0)
    size = half + 2 * edge
    step = 16
    for held, out in ((own_w, out_own), (near_w, out_near), (slope_w, out_slope)):
        for start in range(0, size, step):
            line = lax.broadcasted_iota(jnp.int32, (step, width), 0) + start
            inside = (line >= jnp.where(even, 0, edge)) & (line < jnp.where(even, size, edge + half))
            out[start : start + step, :] = jnp.where(inside, banded(held, weight_w, start + edge, step), 0.0)


def multiply(visitor, visitor_rim, ends, slope_applied, own_applied, near_applied, curve,
             out_keep, out_send, seen, moved):
    y, h, basis = place()
    even = h == 0
    core = lax.rem(basis, 2)
    rows = ends.shape[1]
    half = rows // 2
    size = half + edge
    at_far = (even & (y == 3)) | ((h == 1) & (y == 0))
    at = pl.multiple_of(jnp.where(even, edge, 0), edge)
    seen[0:edge, :] = visitor_rim[0:edge, :]
    seen[size:, :] = visitor_rim[0:edge, :]
    seen[pl.ds(at, size), :] = visitor[...]
    moved[...] = seen[...]

    @pl.when(at_far)
    def _():
        moved[0:edge, :] = visitor_rim[edge : 2 * edge, :]
        moved[pl.ds(at, size), :] = ends[h, pl.ds(pl.multiple_of(h * (half - edge), edge), size), :]

    scale = 1.0 / (2.0 * radial_step)
    view = halves(seen[...])
    cross = product_of_halves(view, halves(slope_applied[...]))
    first = product_of_halves(halves(own_applied[...]), view) * scale
    second = product_of_halves(halves(near_applied[...]), halves(moved[...])) * scale
    low = core == 0
    for index, part in enumerate((cross, curve[...], first, second)):
        part = part.reshape(32, 2 * 4, part.shape[1])
        front, back = part[:, :4, :], part[:, 4:, :]
        out_keep[:, 4 * index : 4 * index + 4, :] = jnp.where(low, front, back)
        out_send[:, 4 * index : 4 * index + 4, :] = jnp.where(low, back, front)


def kernel(body, shapes, scratch, work, *operands):
    return pl.pallas_call(
        body,
        out_shape=[jax.ShapeDtypeStruct(shape, jnp.float32) for shape in shapes],
        scratch_shapes=[pltpu.VMEM(shape, jnp.float32) for shape in scratch],
        compiler_params=pltpu.CompilerParams(vmem_limit_bytes=40 * 1024 * 1024),
        cost_estimate=pl.CostEstimate(flops=work, bytes_accessed=4 * 1024 * 1024, transcendentals=0),
    )(*operands)


def whole(shape):
    return pl.BlockSpec(shape, lambda i: (0,) * len(shape))


def shards(panels, end_panels, correlation_diag, correlation_band, band_reach, sign_rows):
    own = panels[0]
    rows, width = own.shape
    half = rows // 2
    h = lax.axis_index("rho") % 2
    reach = band_reach[None, :]

    half_rows, rim, visitor_rim, picked = pl.pallas_call(
        prepare,
        grid=(1,),
        in_specs=[
            whole(own.shape),
            whole((2, edge, width)),
            pl.BlockSpec((2, edge, width), lambda i: (0, rows // edge - 1, 0)),
            whole(correlation_band.shape),
            whole(band_reach.shape),
            whole(sign_rows.shape),
        ],
        out_specs=[whole((half + edge, width)), whole((3 * edge, width)), whole((2 * edge, width)), whole((8, 1, width))],
        out_shape=[
            jax.ShapeDtypeStruct(shape, jnp.float32)
            for shape in ((half + edge, width), (3 * edge, width), (2 * edge, width), (8, 1, width))
        ],
        compiler_params=pltpu.CompilerParams(vmem_limit_bytes=60 * 1024 * 1024),
        cost_estimate=pl.CostEstimate(flops=1000000, bytes_accessed=2 * 1024 * 1024, transcendentals=0),
    )(own, end_panels, end_panels, correlation_band, band_reach, sign_rows)
    own_rim = move(rim, halo_own)
    picked = spread(picked, z_groups).sum(0)
    near = move(own, to_neighbour)
    half_rows, picked, own_rim, visitor_rim = lax.optimization_barrier((half_rows, picked, own_rim, visitor_rim))
    visitor = move(half_rows, swap_parity)
    visitor_rim = move(visitor_rim, halo_visitor)
    own_sum = gather_sum(picked, plane_groups)
    near_rim = move(jnp.concatenate([own_rim[:edge], jnp.broadcast_to(own_sum, (edge, width))]), to_neighbour)

    window = half + 4 * edge
    frame = rows + 4 * edge
    slope_applied, own_applied, near_applied, curve = kernel(
        apply,
        [(half + 2 * edge, width)] * 3 + [(width, width)],
        [(frame, width)] * 3
        + [(frame, 2 * edge), (2 * edge, rows), (frame - 2 * edge, width)]
        + [(window, width)] * 3
        + [(window, 2 * edge)],
        1000000000,
        own, near, end_panels, own_rim, near_rim, own_sum, correlation_diag[None, :], correlation_band, reach,
    )
    keep, send = kernel(
        multiply,
        [(32, 16, width)] * 2,
        [(half + 2 * edge, width)] * 2,
        1000000000,
        visitor, visitor_rim, end_panels, slope_applied, own_applied, near_applied, curve,
    )
    mine = keep + move(send, swap_core)
    mine = spread(mine.reshape(4, 8, 16, width), x_groups).sum(0)
    mine = spread(mine, z_groups).sum(0)
    y, basis = lax.axis_index("rho") // 2, lax.axis_index("basis")
    at_far = jnp.where(h == 0, y == 3, y == 0)
    line = jnp.arange(edge)[:, None]
    signs = jnp.where(line == 0, jnp.sign(own_sum), jnp.where(at_far, 1.0, jnp.sign(near_rim[edge:])))
    away = move(jnp.concatenate([mine[:8], signs]), swap_parity)
    second = move(mine[8:], from_neighbour)[4:]
    turn = jnp.where(h == 0, 1.0, -1.0)
    here = lax.dynamic_slice_in_dim(signs[0], basis * 4, 4)[:, None]
    drift = turn * (mine[8:12] * away[8] - second * away[9]) + here * away[:4]
    return jnp.stack([drift, away[4:8]], axis=1)[:, None]


def solution(mesh):
    in_specs = (
        P("rho", "basis", None),
        P(None, "basis", None),
        P("basis"),
        P(None, "basis"),
        P("basis"),
        P("rho", None),
    )
    out_specs = P("basis", "rho", None, None)
    return jax.shard_map(shards, mesh=mesh, in_specs=in_specs, out_specs=out_specs, check_vma=False)
```
